128 devices in a mesh: micro: 8 (over y_lo, z), grid: 16 (over y_hi, x, core).
Axes of the slice: x: 4, y: 4 (y_hi: 2, y_lo: 2; y = y_hi * 2 + y_lo), z: 4, core: 2. Of those that a mesh axis runs over, the one named last changes fastest.
Arguments:
- orbitals: float32 [2, 64, 64, 16, 256], P(None, 'micro', None, 'grid'), may hold values from -14 to 14
- local_potential: float32 [64, 16, 256], P('micro', 'grid'), may hold values from -1 to 1
- projectors: float32 [2, 32, 16, 256], P(None, None, 'grid'), may hold values from -0.09375 to 0.09375
- strengths: float32 [2, 32], replicated, may hold values from 1 to 12
- material: int32 [64], replicated, may hold values from 0 to 1
- proj_kind: int32 [64], replicated, may hold values from 0 to 1
- point_cell: int32 [64], replicated, may hold values from 0 to 1999
- vector_now: float32 [2000], replicated, may hold values from -3 to 3
- vector_old: float32 [2000], replicated, may hold values from -3 to 3
Outputs:
- orbitals_out: float32 [2, 64, 64, 16, 256], P(None, 'micro', None, 'grid')
- vector_field: float32 [2000], replicated
The draws below stay inside these ranges and needn't reach their ends.
All inputs are finite; a program needn't handle non-finite values.
Results may differ from the reference program's by a relative error of at most 0.0003.
Values sent between devices are 32-bit elements; how exact they have to be, the bound alone decides.
No kernel may reach another device: no remote copies, remote signals or barrier semaphores. Data moves between devices by JAX's collectives and lax.ppermute only.
A program may use at most 128 MiB of HBM per device.

```python
import math
import jax
import jax.numpy as jnp
from jax import lax

NX = 16
NY = 16
NZ = 16
ORB = 64
NPROJ = 32
KINDS = 2
POINTS = 64
MACRO_CELLS = 2000
STEPS = 2
ORDER = 4


def draw_orbitals(key, part):
    subkeys = jax.random.split(key, 3)
    cells = NY * NZ
    z_index = (jnp.arange(cells, dtype=jnp.int32) % NZ).astype(jnp.float32)
    wave_modes = jax.random.randint(subkeys[0], (POINTS, ORB, 1, 1), 1, NZ // 4 + 1).astype(jnp.float32)
    phases = jax.random.uniform(subkeys[1], (POINTS, ORB, 1, 1), minval=-math.pi, maxval=math.pi)
    angular_offset = 2.0 * math.pi * wave_modes * z_index / NZ + phases
    planes = jnp.arange(NX).astype(jnp.float32)
    growing_amplitude = (3.0 ** (planes / (NX - 1))).reshape(1, 1, NX, 1)
    large_scale_share = 0.6 * jnp.clip(jax.random.normal(subkeys[2], (2, POINTS, ORB, NX, cells)), -6.0, 6.0)
    scaling_coefficient = jnp.ones((POINTS, ORB, 1, 1), jnp.float32)
    oscillating_cosine = jnp.stack([jnp.cos(angular_offset), jnp.sin(angular_offset)])
    return (growing_amplitude * scaling_coefficient * (oscillating_cosine + large_scale_share)).astype(jnp.float32)


def with_ends(drawn, stream_key, low, top_value):
    shape = drawn.shape
    index_at = [jax.random.randint(jax.random.fold_in(stream_key, axis), (), 0, shape[axis]) for axis in range(len(shape))]
    drawn = drawn.at[tuple(index_at)].set(low)
    longest = shape.index(max(shape))
    index_at[longest] = (index_at[longest] + 1) % shape[longest]
    return drawn.at[tuple(index_at)].set(top_value)


def block_levels(stream_key, shape, cuts, low, largest):
    def one(dim, parts):
        steps = jax.random.uniform(jax.random.fold_in(jax.random.fold_in(stream_key, 6), dim), (parts,), jnp.float32, low / len(cuts), largest / len(cuts))
        return jnp.repeat(jnp.exp(steps), shape[dim] // parts).reshape((-1,) + (1,) * (len(shape) - dim - 1))

    gain = one(*cuts[0])
    for cut in cuts[1:]:
        gain = gain * one(*cut)
    return gain


def noise(stream_key, shape, width, reach, pieces=(), kind=jnp.bfloat16):
    values = jax.random.normal(stream_key, shape, jnp.float32) * width
    if len(pieces) > 0:
        values = block_levels(stream_key, shape, pieces, -0.22, 0.18) * values
    return jnp.clip(values, min=-reach, max=reach).astype(kind)


def setup_inputs(seed: int = 0) -> dict:
    keys = jax.random.split(jax.random.key(seed), 10)
    return {
        "orbitals": draw_orbitals(jax.random.fold_in(keys[9], 71), 0),
        "local_potential": jnp.clip(jax.random.uniform(keys[1], (POINTS, NX, NY * NZ), jnp.float32, -1.0, 1.0) * block_levels(keys[1], (POINTS, NX, NY * NZ), ((0, 8), (1, 16)), -0.4, 0.0), -1.0, 1.0),
        "projectors": noise(keys[2], (KINDS, NPROJ, NX, NY * NZ), (NX * NY * NZ) ** -0.5, 0.09375, ((2, 16),), jnp.float32),
        "strengths": jnp.clip(jnp.exp(jax.random.uniform(keys[3], (KINDS, NPROJ), jnp.float32, math.log(1.0), math.log(12.0))), 1.0, 12.0),
        "material": with_ends(jax.random.randint(keys[4], (POINTS,), 0, 2), jax.random.fold_in(keys[4], 1), 0, 1).astype(jnp.int32),
        "proj_kind": with_ends(jax.random.randint(keys[5], (POINTS,), 0, KINDS), jax.random.fold_in(keys[5], 1), 0, KINDS - 1).astype(jnp.int32),
        "point_cell": with_ends(jax.random.randint(keys[6], (POINTS,), 0, MACRO_CELLS), jax.random.fold_in(keys[6], 1), 0, MACRO_CELLS - 1).astype(jnp.int32),
        "vector_now": noise(keys[7], (MACRO_CELLS,), 0.5, 3.0, (), jnp.float32),
        "vector_old": noise(keys[8], (MACRO_CELLS,), 0.5, 3.0, (), jnp.float32),
    }


SPACING = 0.64
TIME_STEP = 0.05
COURANT = 0.9
COUPLING = 1.0
HIGHEST = lax.Precision.HIGHEST


def z_gradient(field):
    extent = field.shape
    blocks = field.reshape(extent[:-1] + (NY, NZ))
    change = jnp.roll(blocks, -1, len(extent)) - jnp.roll(blocks, 1, len(extent))
    return change.reshape(extent) / (2.0 * SPACING)


def neighbour_sums(field):
    extent = field.shape
    blocks = field.reshape(extent[:-1] + (NY, NZ))
    horizontal_direction = jnp.roll(blocks, 1, 3) + jnp.roll(blocks, -1, 3)
    along_y = jnp.roll(blocks, 1, 4) + jnp.roll(blocks, -1, 4)
    forward = jnp.roll(blocks, -1, 5)
    backward = jnp.roll(blocks, 1, 5)
    beside_all = (horizontal_direction + along_y + forward + backward).reshape(extent)
    field_gradient = (forward - backward).reshape(extent) / (2.0 * SPACING)
    return beside_all, field_gradient


def apply_hamiltonian(field, field_at, potential, beta_flat, weights):
    beside_all, field_gradient = neighbour_sums(field)
    diagonal = 3.0 / SPACING ** 2 + 0.5 * field_at * field_at + potential
    kinetic = diagonal * field - beside_all / (2.0 * SPACING ** 2)
    drift = jnp.stack([field_gradient[1], -field_gradient[0]]) * field_at
    flattened_rows = field.reshape(-1, beta_flat.shape[1])
    intersection = jnp.dot(flattened_rows, beta_flat.T, precision=HIGHEST)
    intersection = intersection.reshape(field.shape[:3] + (-1,)) * weights[None, :, None, :]
    nonlocal_part = jnp.dot(intersection.reshape(flattened_rows.shape[0], -1), beta_flat, precision=HIGHEST)
    return kinetic + drift + nonlocal_part.reshape(field.shape)


def point_current(field, field_at, occupied):
    field_gradient = z_gradient(field)
    flow = field[0] * field_gradient[1] - field[1] * field_gradient[0]
    density = field[0] * field[0] + field[1] * field[1]
    per_orbital = jnp.sum(flow + field_at * density, axis=(2, 3))
    return jnp.sum(per_orbital * occupied, axis=1) * (2.0 / (ORB * NX * NY * NZ))


def reference(orbitals, local_potential, projectors, strengths, material, proj_kind, point_cell, vector_now, vector_old):
    beta_flat = projectors.reshape(KINDS * NPROJ, NX * NY * NZ)
    kind_onehot = (proj_kind[:, None] == jnp.arange(KINDS, dtype=jnp.int32)[None, :]).astype(jnp.float32)
    weights = (kind_onehot[:, :, None] * strengths[None]).reshape(POINTS, KINDS * NPROJ)
    orbital_ids = jnp.arange(ORB, dtype=jnp.int32)
    occupied = ((orbital_ids[None, :] < ORB // 2) | (material[:, None] == 1)).astype(jnp.float32)
    potential = local_potential[:, None]
    macro_ids = jnp.arange(MACRO_CELLS, dtype=jnp.int32)
    placement = (point_cell[:, None] == macro_ids[None, :]).astype(jnp.float32)
    field = orbitals
    present = vector_now
    previous = vector_old
    for step_index in range(STEPS):
        field_at = present[point_cell].reshape(POINTS, 1, 1, 1)
        summed = field
        taylor_term = field
        for degree in range(1, ORDER + 1):
            applied = apply_hamiltonian(taylor_term, field_at, potential, beta_flat, weights)
            taylor_term = (TIME_STEP / degree) * jnp.stack([applied[1], -applied[0]])
            summed = summed + taylor_term
        field = summed
        currents = point_current(field, field_at, occupied)
        accumulate_current = jnp.dot(currents, placement, precision=HIGHEST)
        extended_with_zeros = jnp.pad(present, 1)
        curvature = extended_with_zeros[2:] + extended_with_zeros[:-2] - 2.0 * present
        following = 2.0 * present - previous + COURANT ** 2 * curvature - COUPLING * accumulate_current
        previous = present
        present = following
    return field * occupied[None, :, :, None, None], present
```

```python
import functools

import jax
import jax.numpy as jnp
from jax import lax
from jax.experimental import pallas as pl
from jax.experimental.pallas import tpu as pltpu
from jax.sharding import PartitionSpec as P

ORB = 64
STEPS = 2
ORDER = 4
SPACING = 0.64
TIME_STEP = 0.05
COURANT = 0.9
COUPLING = 1.0

GRID = 16
LOCAL = 8
HALF = 32
CELLS = 4096
NPROJ = 32
LANES = 128
WIDTH = 2 * LANES
PAYLOAD = 200
MACRO_ROWS = 16
KINETIC = TIME_STEP / (2.0 * SPACING**2)
F32 = jnp.float32
BF16 = jnp.bfloat16
VMEM = pl.BlockSpec(memory_space=pltpu.VMEM)
SMEM = pl.BlockSpec(memory_space=pltpu.SMEM)


def split(value):
    high = value.astype(BF16)
    low = (value - high.astype(F32)).astype(BF16)
    return high, low


def dot(a, b):
    return jnp.dot(a, b, preferred_element_type=F32)


def pack_kernel(kind_ref, x_ref, proj_ref, pot_ref, out_ref):
    first = lax.axis_index("micro") * LOCAL
    for p in range(LOCAL):
        kind = kind_ref[first + p]
        for h in range(2):
            g = 2 * p + h
            for half in range(2):
                for ri in range(2):
                    row = half * 64 + ri * 32
                    out_ref[g, row : row + 32, :] = x_ref[ri, p, h, pl.ds(half, 32, stride=2), :]
                row = 128 + half * 32
                out_ref[g, row : row + 32, :] = proj_ref[kind, pl.ds(half, 32, stride=2), :]
            out_ref[g, 192:200, :] = jnp.broadcast_to(pot_ref[2 * p : 2 * p + 1, :], (8, LANES))
            out_ref[g, 193:194, :] = pot_ref[2 * p + 1 : 2 * p + 2, :]


def turned(block, turn_ref, slot):
    turn_ref[slot] = block.T
    even = turn_ref[slot, pl.ds(0, 64, stride=2), :].reshape(8, 8, LANES)
    odd = turn_ref[slot, pl.ds(1, 64, stride=2), :].reshape(8, 8, LANES)
    return jnp.concatenate([even, odd], axis=1)


def unpack(recv_ref, term_ref, sum_ref, pieces_ref, diag_ref, beta_ref, rows_ref, columns_ref, turn_ref):
    for x in range(4):
        for half in range(2):
            y = pl.ds(half * 8, 8)
            for ri in range(2):
                row = half * 64 + ri * 32
                block = jnp.concatenate([recv_ref[4 * k + x, row : row + 32, :] for k in range(4)], axis=0)
                tile = turned(block, turn_ref, ri)
                term_ref[0, ri, y, x] = tile
                sum_ref[ri, y, x] = tile
                high, low = split(tile)
                lanes = slice(ri * LANES, (ri + 1) * LANES)
                pieces_ref[0, y, x, :, lanes] = high
                pieces_ref[1, y, x, :, lanes] = low
            row = 192 + half
            block = jnp.concatenate(
                [jnp.broadcast_to(recv_ref[4 * k + x, row : row + 1, :], (32, LANES)) for k in range(4)], axis=0
            )
            diag_ref[y, x] = TIME_STEP * (3.0 / SPACING**2 + turned(block, turn_ref, 2))
            row = 128 + half * 32
            block = jnp.concatenate([recv_ref[4 * k + x, row : row + 32, :] for k in range(4)], axis=0)
            tile = turned(block, turn_ref, 3)
            beta_ref[y, x] = tile
            high, low = split(tile)
            rows_ref[y, x, :, 0:128] = high
            rows_ref[y, x, :, 128:256] = low
            rows_ref[y, x, :, 256:384] = high
    for b in range(8):
        block = beta_ref[2 * b : 2 * b + 2].reshape(LANES, LANES).T
        high, low = split(block)
        columns_ref[0:128, b * LANES : (b + 1) * LANES] = high
        columns_ref[128:256, b * LANES : (b + 1) * LANES] = low


def propagate(a, weight, term_ref, sum_ref, pieces_ref, diag_ref, rows_ref, columns_ref, nonlocal_ref, coef_ref):
    diag_shift = TIME_STEP * 0.5 * a * a
    drift = a * (TIME_STEP / (2.0 * SPACING))
    group_of_lane = lax.broadcasted_iota(jnp.int32, (NPROJ, WIDTH), 1) % LANES // 32

    def order(n, _):
        now = (n + 1) % 2
        later = n % 2
        scale = jnp.where(n == 1, 1.0, jnp.where(n == 2, 1.0 / 2, jnp.where(n == 3, 1.0 / 3, 1.0 / 4))).astype(F32)
        high = pieces_ref[0].reshape(1024, WIDTH)
        low = pieces_ref[1].reshape(1024, WIDTH)
        both = dot(columns_ref[...], high)
        coef = both[0:128] + both[128:256] + dot(columns_ref[0:128], low)
        mine = jnp.zeros((NPROJ, WIDTH), F32)
        for k in range(4):
            mine = mine + jnp.where(group_of_lane == k, coef[k * 32 : k * 32 + 32], 0.0)
        parts = []
        for ri in range(2):
            part = mine[:, ri * LANES : (ri + 1) * LANES]
            part = part + pltpu.roll(part, 64, 1)
            part = part + pltpu.roll(part, 32, 1)
            parts.append(part)
        mine = jnp.concatenate(parts, axis=1) * weight
        for k in range(4):
            high, low = split(jnp.where(group_of_lane == k, mine, 0.0))
            coef_ref[k * 32 : k * 32 + 32, :] = high
            coef_ref[128 + k * 32 : 128 + k * 32 + 32, :] = high
            coef_ref[256 + k * 32 : 256 + k * 32 + 32, :] = low
        nonlocal_ref[...] = dot(rows_ref[...].reshape(1024, 384), coef_ref[...]).reshape(16, 4, 16, WIDTH)

        def row(y, _):
            above = (y + 1) % 16
            below = (y + 15) % 16
            centre = [[term_ref[now, ri, y, x] for x in range(4)] for ri in range(2)]
            for x in range(4):
                diag = diag_ref[y, x] + diag_shift
                kinetic, gradient = [], []
                for ri in range(2):
                    c = centre[ri][x]
                    right = centre[ri][x + 1] if x < 3 else pltpu.roll(centre[ri][0], 96, 1)
                    left = centre[ri][x - 1] if x > 0 else pltpu.roll(centre[ri][3], 32, 1)
                    across = right + left + (term_ref[now, ri, above, x] + term_ref[now, ri, below, x])
                    even, odd = c[0:8], c[8:16]
                    before = pltpu.roll(odd, 1, 0)
                    after = pltpu.roll(even, 7, 0)
                    around = across + jnp.concatenate([odd + before, after + even], axis=0)
                    gradient.append(jnp.concatenate([odd - before, after - even], axis=0))
                    there = nonlocal_ref[y, x, :, ri * LANES : (ri + 1) * LANES]
                    kinetic.append(diag * c - KINETIC * around + there)
                new = [
                    scale * (kinetic[1] - drift * gradient[0]),
                    scale * (-kinetic[0] - drift * gradient[1]),
                ]
                for ri in range(2):
                    term_ref[later, ri, y, x] = new[ri]
                    sum_ref[ri, y, x] = sum_ref[ri, y, x] + new[ri]
                    high, low = split(new[ri])
                    lanes = slice(ri * LANES, (ri + 1) * LANES)
                    pieces_ref[0, y, x, :, lanes] = high
                    pieces_ref[1, y, x, :, lanes] = low
            return 0

        lax.fori_loop(0, 16, row, 0)
        return 0

    lax.fori_loop(1, ORDER + 1, order, 0)


def partial_current(a, sum_ref):
    def row(y, total):
        for x in range(4):
            real, imag = sum_ref[0, y, x], sum_ref[1, y, x]
            real_even, real_odd = real[0:8], real[8:16]
            imag_even, imag_odd = imag[0:8], imag[8:16]
            flow = real_even * imag_odd - imag_even * real_odd
            flow = flow + (real_odd * pltpu.roll(imag_even, 7, 0) - imag_odd * pltpu.roll(real_even, 7, 0))
            square = real * real + imag * imag
            total = total + (flow * (1.0 / SPACING) + a * (square[0:8] + square[8:16]))
        return total

    total = lax.fori_loop(0, 16, row, jnp.zeros((8, LANES), F32))
    total = jnp.sum(jnp.sum(total, axis=0, keepdims=True), axis=1, keepdims=True)
    return total * (2.0 / (ORB * CELLS))


def my_point():
    return lax.axis_index("micro") * LOCAL + lax.axis_index("grid") // 2


def is_occupied(material_ref):
    return jnp.logical_or(lax.axis_index("grid") % 2 == 0, material_ref[my_point()] == 1)


def projector_weight(kind_ref, strength_ref):
    kind = kind_ref[my_point()]
    row = jnp.where(kind == 0, strength_ref[0:1, :], strength_ref[1:2, :])
    across = lax.broadcasted_iota(jnp.int32, (NPROJ, NPROJ), 1)
    down = lax.broadcasted_iota(jnp.int32, (NPROJ, NPROJ), 0)
    return TIME_STEP * jnp.sum(jnp.where(across == down, row, 0.0), axis=1, keepdims=True)


def first_kernel(
    kind_ref, cell_ref, material_ref, vector_ref, strength_ref, recv_ref,
    sum_ref, diag_ref, rows_ref, columns_ref, part_ref,
    term_ref, pieces_ref, beta_ref, turn_ref, nonlocal_ref, coef_ref,
):
    unpack(recv_ref, term_ref, sum_ref, pieces_ref, diag_ref, beta_ref, rows_ref, columns_ref, turn_ref)
    a = vector_ref[cell_ref[my_point()]]
    weight = projector_weight(kind_ref, strength_ref)
    propagate(a, weight, term_ref, sum_ref, pieces_ref, diag_ref, rows_ref, columns_ref, nonlocal_ref, coef_ref)
    part = jnp.where(is_occupied(material_ref), partial_current(a, sum_ref), 0.0)
    part_ref[...] = jnp.broadcast_to(part, (LANES, LANES))


def macro_index():
    down = lax.broadcasted_iota(jnp.int32, (MACRO_ROWS, LANES), 0)
    return down * LANES + lax.broadcasted_iota(jnp.int32, (MACRO_ROWS, LANES), 1)


def next_vector(cell_ref, gathered_ref, present, previous, cells):
    index = macro_index()
    deposit = jnp.zeros((MACRO_ROWS, LANES), F32)
    for point in range(64):
        current = gathered_ref[2 * point : 2 * point + 1, :] + gathered_ref[2 * point + 1 : 2 * point + 2, :]
        deposit = deposit + jnp.where(index == cell_ref[point], current, 0.0)
    lane = lax.broadcasted_iota(jnp.int32, (MACRO_ROWS, LANES), 1)
    zero_row = jnp.zeros((1, LANES), F32)
    back = pltpu.roll(present, 1, 1)
    back = jnp.where(lane == 0, jnp.concatenate([zero_row, back[:-1]], axis=0), back)
    forth = pltpu.roll(present, LANES - 1, 1)
    forth = jnp.where(lane == LANES - 1, jnp.concatenate([forth[1:], zero_row], axis=0), forth)
    curvature = forth + back - 2.0 * present
    following = 2.0 * present - previous + COURANT**2 * curvature - COUPLING * deposit
    return jnp.where(index < cells, following, 0.0)


def second_kernel(
    cells,
    kind_ref, cell_ref, material_ref, strength_ref, gathered_ref, now_ref, old_ref,
    field_ref, diag_ref, rows_ref, columns_ref,
    out_ref, vector_ref, part_ref,
    term_ref, sum_ref, pieces_ref, turn_ref, nonlocal_ref, coef_ref,
):
    following = next_vector(cell_ref, gathered_ref, now_ref[...], old_ref[...], cells)
    vector_ref[...] = following
    mine = jnp.where(macro_index() == cell_ref[my_point()], following, 0.0)
    a = jnp.sum(jnp.sum(mine, axis=0, keepdims=True), axis=1, keepdims=True)
    weight = projector_weight(kind_ref, strength_ref)
    for ri in range(2):
        for x in range(4):
            tile = field_ref[ri, :, x]
            term_ref[0, ri, :, x] = tile
            sum_ref[ri, :, x] = tile
            high, low = split(tile)
            lanes = slice(ri * LANES, (ri + 1) * LANES)
            pieces_ref[0, :, x, :, lanes] = high
            pieces_ref[1, :, x, :, lanes] = low
    propagate(a, weight, term_ref, sum_ref, pieces_ref, diag_ref, rows_ref, columns_ref, nonlocal_ref, coef_ref)
    occupied = is_occupied(material_ref)
    part = jnp.where(occupied, partial_current(a, sum_ref), 0.0)
    part_ref[...] = jnp.broadcast_to(part, (LANES, LANES))
    keep = jnp.where(occupied, 1.0, 0.0).astype(F32)
    for x in range(4):
        for half in range(2):
            for ri in range(2):
                tile = sum_ref[ri, pl.ds(half * 8, 8), x] * keep
                turn_ref[ri, pl.ds(0, 64, stride=2), :] = tile[:, 0:8].reshape(64, LANES)
                turn_ref[ri, pl.ds(1, 64, stride=2), :] = tile[:, 8:16].reshape(64, LANES)
                block = turn_ref[ri].T
                for k in range(4):
                    out_ref[4 * k + x, pl.ds(ri * 64 + half, 32, stride=2), :] = block[k * 32 : k * 32 + 32]


def last_kernel(cells, cell_ref, gathered_ref, now_ref, old_ref, out_ref):
    out_ref[...] = next_vector(cell_ref, gathered_ref, now_ref[...], old_ref[...], cells)


FIELD = (2, 16, 4, 16, LANES)
PARAMS = pltpu.CompilerParams(vmem_limit_bytes=24 * 2**20)


def local(
    orbitals,
    local_potential,
    projectors,
    strengths,
    material,
    proj_kind,
    point_cell,
    vector_now,
    vector_old,
):
    cells = vector_now.shape[0]
    shape = jax.ShapeDtypeStruct
    packed = pl.pallas_call(
        pack_kernel,
        out_shape=shape((GRID, PAYLOAD, LANES), F32),
        in_specs=[SMEM, VMEM, VMEM, VMEM],
        out_specs=VMEM,
        compiler_params=PARAMS,
        name="pack",
    )(
        proj_kind,
        orbitals.reshape(2, LOCAL, 2, 64, LANES),
        projectors.reshape(2, 64, LANES),
        local_potential.reshape(16, LANES),
    )
    received = lax.all_to_all(packed, "grid", split_axis=0, concat_axis=0, tiled=True)
    working = [
        pltpu.VMEM((2,) + FIELD, F32),
        pltpu.VMEM((2, 16, 4, 16, WIDTH), BF16),
        pltpu.VMEM(FIELD[1:], F32),
        pltpu.VMEM((4, LANES, LANES), F32),
        pltpu.VMEM((16, 4, 16, WIDTH), F32),
        pltpu.VMEM((384, WIDTH), BF16),
    ]
    field, diag, rows, columns, part = pl.pallas_call(
        first_kernel,
        out_shape=[
            shape(FIELD, F32),
            shape(FIELD[1:], F32),
            shape((16, 4, 16, 384), BF16),
            shape((256, 1024), BF16),
            shape((LANES, LANES), F32),
        ],
        in_specs=[SMEM] * 4 + [VMEM] * 2,
        out_specs=[VMEM] * 5,
        scratch_shapes=working,
        compiler_params=PARAMS,
        name="first",
    )(proj_kind, point_cell, material, vector_now, strengths, received)

    def gather(part):
        part = part.reshape(LANES, 1, LANES)
        part = lax.all_to_all(part, ("micro", "grid"), split_axis=0, concat_axis=0, tiled=True)
        return part.reshape(LANES, LANES)

    macro = MACRO_ROWS * LANES
    now = jnp.pad(vector_now, (0, macro - cells)).reshape(MACRO_ROWS, LANES)
    old = jnp.pad(vector_old, (0, macro - cells)).reshape(MACRO_ROWS, LANES)
    out, following, part = pl.pallas_call(
        functools.partial(second_kernel, cells),
        out_shape=[
            shape((GRID, LANES, LANES), F32),
            shape((MACRO_ROWS, LANES), F32),
            shape((LANES, LANES), F32),
        ],
        in_specs=[SMEM] * 3 + [VMEM] * 8,
        out_specs=[VMEM] * 3,
        scratch_shapes=[working[0], pltpu.VMEM(FIELD, F32), working[1]] + working[3:],
        compiler_params=PARAMS,
        name="second",
    )(proj_kind, point_cell, material, strengths, gather(part), now, old, field, diag, rows, columns)
    out = lax.all_to_all(out, "grid", split_axis=0, concat_axis=0, tiled=True)
    last = pl.pallas_call(
        functools.partial(last_kernel, cells),
        out_shape=shape((MACRO_ROWS, LANES), F32),
        in_specs=[SMEM] + [VMEM] * 3,
        out_specs=VMEM,
        compiler_params=PARAMS,
        name="last",
    )(point_cell, gather(part), following, now)
    out = out.reshape(LOCAL, 2, 2, 64, LANES).transpose(2, 0, 1, 3, 4)
    return out.reshape(orbitals.shape), last.reshape(macro)[:cells]


def solution(mesh):
    in_specs = (
        P(None, "micro", None, "grid", None),
        P("micro", "grid", None),
        P(None, None, "grid", None),
        P(),
        P(),
        P(),
        P(),
        P(),
        P(),
    )
    out_specs = (P(None, "micro", None, "grid", None), P())
    return jax.shard_map(local, mesh=mesh, in_specs=in_specs, out_specs=out_specs, check_vma=False)
```

```python
import functools

import jax
import jax.numpy as jnp
from jax import lax
from jax.experimental import pallas as pl
from jax.experimental.pallas import tpu as pltpu
from jax.sharding import PartitionSpec as P

ORB = 64
STEPS = 2
ORDER = 4
SPACING = 0.64
TIME_STEP = 0.05
COURANT = 0.9
COUPLING = 1.0

GRID = 16
LOCAL = 8
HALF = 32
CELLS = 4096
NPROJ = 32
LANES = 128
WIDTH = 2 * LANES
PAYLOAD = 168
RETURN = 136
MACRO_ROWS = 16
KINETIC = TIME_STEP / (2.0 * SPACING**2)
F32 = jnp.float32
BF16 = jnp.bfloat16
VMEM = pl.BlockSpec(memory_space=pltpu.VMEM)
SMEM = pl.BlockSpec(memory_space=pltpu.SMEM)
HBM = pl.BlockSpec(memory_space=pltpu.HBM)


def split(value):
    high = value.astype(BF16)
    low = (value - high.astype(F32)).astype(BF16)
    return high, low


def dot(a, b):
    return jnp.dot(a, b, preferred_element_type=F32)


def pack_kernel(kind_hbm, x_hbm, proj_hbm, pot_hbm, out_ref, kind_ref, pot_ref, small_sem, sem):
    kind_copy = pltpu.make_async_copy(kind_hbm, kind_ref, small_sem.at[0])
    pot_copy = pltpu.make_async_copy(pot_hbm, pot_ref, small_sem.at[1])
    kind_copy.start()
    pot_copy.start()
    copies = []
    for p in range(LOCAL):
        for h in range(2):
            for ri in range(2):
                target = out_ref.at[2 * p + h, pl.ds(ri * 64, 64)]
                copies.append(pltpu.make_async_copy(x_hbm.at[ri, p, h], target, sem.at[len(copies)]))
                copies[-1].start()
    kind_copy.wait()
    first = lax.axis_index("micro") * LOCAL
    for p in range(LOCAL):
        kind = kind_ref[first + p]
        for h in range(2):
            target = out_ref.at[2 * p + h, pl.ds(128, 32)]
            copies.append(pltpu.make_async_copy(proj_hbm.at[kind, pl.ds(h * 32, 32)], target, sem.at[len(copies)]))
            copies[-1].start()
    pot_copy.wait()
    for p in range(LOCAL):
        for h in range(2):
            g = 2 * p + h
            out_ref[g, 160:168, :] = jnp.broadcast_to(pot_ref[2 * p : 2 * p + 1, :], (8, LANES))
            out_ref[g, 161:162, :] = pot_ref[2 * p + 1 : 2 * p + 2, :]
    for copy in copies:
        copy.wait()


def turned(block, turn_ref, slot):
    turn_ref[slot] = block.T
    even = turn_ref[slot, pl.ds(0, 64, stride=2), :].reshape(8, 8, LANES)
    odd = turn_ref[slot, pl.ds(1, 64, stride=2), :].reshape(8, 8, LANES)
    return jnp.concatenate([even, odd], axis=1)


def unpack_kernel(recv_ref, u_ref, pieces_ref, diag_ref, turn_ref):
    for x in range(4):
        for half in range(2):
            y = pl.ds(half * 8, 8)
            for ri in range(2):
                rows = pl.ds(ri * 64 + half, 32, stride=2)
                block = jnp.concatenate([recv_ref[4 * k + x, rows, :] for k in range(4)], axis=0)
                tile = turned(block, turn_ref, (2 * x + half) % 2 * 3 + ri)
                u_ref[ri, y, x] = tile
                high, low = split(tile)
                lanes = slice(ri * LANES, (ri + 1) * LANES)
                pieces_ref[0, y, x, :, lanes] = high
                pieces_ref[1, y, x, :, lanes] = low
            row = 160 + half
            block = jnp.concatenate(
                [jnp.broadcast_to(recv_ref[4 * k + x, row : row + 1, :], (32, LANES)) for k in range(4)], axis=0
            )
            tile = turned(block, turn_ref, (2 * x + half) % 2 * 3 + 2)
            diag_ref[y, x] = TIME_STEP * (3.0 / SPACING**2 + tile)


def unpack_projectors(recv_ref, other_ref, beta_ref, rows_ref, columns_ref, turn_ref):
    for x in range(4):
        for half in range(2):
            y = pl.ds(half * 8, 8)
            own, other = pl.ds(128 + half, 16, stride=2), pl.ds(half, 16, stride=2)
            block = []
            for k in range(4):
                block += [recv_ref[4 * k + x, own, :], other_ref[4 * k + x, other, :]]
            tile = turned(jnp.concatenate(block, axis=0), turn_ref, 2 * (x % 2) + half)
            beta_ref[y, x] = tile
            high, low = split(tile)
            rows_ref[y, x, :, 0:128] = high
            rows_ref[y, x, :, 128:256] = low
            rows_ref[y, x, :, 256:384] = high
    for b in range(8):
        block = beta_ref[2 * b : 2 * b + 2].reshape(LANES, LANES).T
        high, low = split(block)
        columns_ref[0:128, b * LANES : (b + 1) * LANES] = high
        columns_ref[128:256, b * LANES : (b + 1) * LANES] = low


def apply(scale, a, weight, u_ref, term_ref, out_ref, pieces_in, pieces_out, diag_ref, rows_ref, columns_ref, nonlocal_ref, coef_ref, current):
    diag_shift = TIME_STEP * 0.5 * a * a
    drift = a * (TIME_STEP / (2.0 * SPACING))
    group_of_lane = lax.broadcasted_iota(jnp.int32, (NPROJ, WIDTH), 1) % LANES // 32
    high = pieces_in[0].reshape(1024, WIDTH)
    low = pieces_in[1].reshape(1024, WIDTH)
    both = dot(columns_ref[...], high)
    coef = both[0:128] + both[128:256] + dot(columns_ref[0:128], low)
    mine = jnp.zeros((NPROJ, WIDTH), F32)
    for k in range(4):
        mine = mine + jnp.where(group_of_lane == k, coef[k * 32 : k * 32 + 32], 0.0)
    parts = []
    for ri in range(2):
        part = mine[:, ri * LANES : (ri + 1) * LANES]
        part = part + pltpu.roll(part, 64, 1)
        part = part + pltpu.roll(part, 32, 1)
        parts.append(part)
    mine = jnp.concatenate(parts, axis=1) * weight
    for k in range(4):
        high, low = split(jnp.where(group_of_lane == k, mine, 0.0))
        coef_ref[k * 32 : k * 32 + 32, :] = high
        coef_ref[128 + k * 32 : 128 + k * 32 + 32, :] = high
        coef_ref[256 + k * 32 : 256 + k * 32 + 32, :] = low

    def row(y, total):
        above = (y + 1) % 16
        below = (y + 15) % 16
        centre = [[term_ref[ri, y, x] for x in range(4)] for ri in range(2)]
        for x in range(4):
            diag = diag_ref[y, x] + diag_shift
            kinetic, gradient = [], []
            for ri in range(2):
                c = centre[ri][x]
                right = centre[ri][x + 1] if x < 3 else pltpu.roll(centre[ri][0], 96, 1)
                left = centre[ri][x - 1] if x > 0 else pltpu.roll(centre[ri][3], 32, 1)
                across = right + left + (term_ref[ri, above, x] + term_ref[ri, below, x])
                even, odd = c[0:8], c[8:16]
                before = pltpu.roll(odd, 1, 0)
                after = pltpu.roll(even, 7, 0)
                around = across + jnp.concatenate([odd + before, after + even], axis=0)
                gradient.append(jnp.concatenate([odd - before, after - even], axis=0))
                there = nonlocal_ref[y, x, :, ri * LANES : (ri + 1) * LANES]
                kinetic.append(diag * c - KINETIC * around + there)
            new = [
                u_ref[0, y, x] + scale * (kinetic[1] - drift * gradient[0]),
                u_ref[1, y, x] - scale * (kinetic[0] + drift * gradient[1]),
            ]
            for ri in range(2):
                out_ref[ri, y, x] = new[ri]
                if pieces_out is not None:
                    high, low = split(new[ri])
                    lanes = slice(ri * LANES, (ri + 1) * LANES)
                    pieces_out[0, y, x, :, lanes] = high
                    pieces_out[1, y, x, :, lanes] = low
            if current:
                real, imag = new
                real_even, real_odd = real[0:8], real[8:16]
                imag_even, imag_odd = imag[0:8], imag[8:16]
                flow = real_even * imag_odd - imag_even * real_odd
                flow = flow + (real_odd * pltpu.roll(imag_even, 7, 0) - imag_odd * pltpu.roll(real_even, 7, 0))
                square = real * real + imag * imag
                total = total + (flow * (1.0 / SPACING) + a * (square[0:8] + square[8:16]))
        return total

    for chunk in range(4):
        ys = pl.ds(4 * chunk, 4)
        nonlocal_ref[ys] = dot(rows_ref[ys].reshape(256, 384), coef_ref[...]).reshape(4, 4, 16, WIDTH)
    total = jnp.zeros((8, LANES), F32)
    for y in range(16):
        total = row(y, total)
    if current:
        total = jnp.sum(jnp.sum(total, axis=0, keepdims=True), axis=1, keepdims=True)
        return total * (2.0 / (ORB * CELLS))


def propagate(a, weight, u_ref, out_ref, pieces_first, pieces_last, term_refs, pieces_ref, *others):
    one, two = term_refs
    apply(1.0 / 4, a, weight, u_ref, u_ref, one, pieces_first, pieces_ref, *others, False)
    apply(1.0 / 3, a, weight, u_ref, one, two, pieces_ref, pieces_ref, *others, False)
    apply(1.0 / 2, a, weight, u_ref, two, one, pieces_ref, pieces_ref, *others, False)
    return apply(1.0, a, weight, u_ref, one, out_ref, pieces_ref, pieces_last, *others, True)


def my_point():
    return lax.axis_index("micro") * LOCAL + lax.axis_index("grid") // 2


def is_occupied(material_ref):
    return jnp.logical_or(lax.axis_index("grid") % 2 == 0, material_ref[my_point()] == 1)


def projector_weight(kind_ref, strength_ref):
    kind = kind_ref[my_point()]
    row = jnp.where(kind == 0, strength_ref[0:1, :], strength_ref[1:2, :])
    across = lax.broadcasted_iota(jnp.int32, (NPROJ, NPROJ), 1)
    down = lax.broadcasted_iota(jnp.int32, (NPROJ, NPROJ), 0)
    down = (down + lax.axis_index("grid") % 2 * (NPROJ // 2)) % NPROJ
    return TIME_STEP * jnp.sum(jnp.where(across == down, row, 0.0), axis=1, keepdims=True)


def first_kernel(
    kind_ref, cell_ref, material_ref, vector_ref, strength_ref, recv_ref, other_ref,
    u_ref, pieces_in, diag_ref,
    out_ref, pieces_out, rows_ref, columns_ref, part_ref,
    one_ref, two_ref, pieces_ref, beta_ref, turn_ref, nonlocal_ref, coef_ref,
):
    unpack_projectors(recv_ref, other_ref, beta_ref, rows_ref, columns_ref, turn_ref)
    a = vector_ref[cell_ref[my_point()]]
    weight = projector_weight(kind_ref, strength_ref)
    others = (diag_ref, rows_ref, columns_ref, nonlocal_ref, coef_ref)
    part = propagate(a, weight, u_ref, out_ref, pieces_in, pieces_out, (one_ref, two_ref), pieces_ref, *others)
    part_ref[...] = jnp.broadcast_to(jnp.where(is_occupied(material_ref), part, 0.0), (LANES, LANES))


def macro_index():
    down = lax.broadcasted_iota(jnp.int32, (MACRO_ROWS, LANES), 0)
    return down * LANES + lax.broadcasted_iota(jnp.int32, (MACRO_ROWS, LANES), 1)


def next_vector(cell_ref, current, present, previous, cells):
    index = macro_index()
    deposit = jnp.zeros((MACRO_ROWS, LANES), F32)
    for point in range(64):
        deposit = deposit + jnp.where(index == cell_ref[point], current(point), 0.0)
    lane = lax.broadcasted_iota(jnp.int32, (MACRO_ROWS, LANES), 1)
    zero_row = jnp.zeros((1, LANES), F32)
    back = pltpu.roll(present, 1, 1)
    back = jnp.where(lane == 0, jnp.concatenate([zero_row, back[:-1]], axis=0), back)
    forth = pltpu.roll(present, LANES - 1, 1)
    forth = jnp.where(lane == LANES - 1, jnp.concatenate([forth[1:], zero_row], axis=0), forth)
    curvature = forth + back - 2.0 * present
    following = 2.0 * present - previous + COURANT**2 * curvature - COUPLING * deposit
    return jnp.where(index < cells, following, 0.0)


def second_kernel(
    cells,
    kind_ref, cell_ref, material_ref, strength_ref, gathered_ref, now_ref, old_ref,
    u_ref, pieces_in, diag_ref, rows_ref, columns_ref,
    out_ref, vector_ref,
    sum_ref, one_ref, two_ref, pieces_ref, turn_ref, nonlocal_ref, coef_ref,
):

    def current(point):
        return gathered_ref[2 * point : 2 * point + 1, :] + gathered_ref[2 * point + 1 : 2 * point + 2, :]

    following = next_vector(cell_ref, current, now_ref[...], old_ref[...], cells)
    vector_ref[...] = following
    mine = jnp.where(macro_index() == cell_ref[my_point()], following, 0.0)
    a = jnp.sum(jnp.sum(mine, axis=0, keepdims=True), axis=1, keepdims=True)
    weight = projector_weight(kind_ref, strength_ref)
    others = (diag_ref, rows_ref, columns_ref, nonlocal_ref, coef_ref)
    part = propagate(a, weight, u_ref, sum_ref, pieces_in, None, (one_ref, two_ref), pieces_ref, *others)
    occupied = is_occupied(material_ref)
    out_ref[:, 128:136, :] = jnp.broadcast_to(jnp.where(occupied, part, 0.0), (GRID, 8, LANES))
    keep = jnp.where(occupied, 1.0, 0.0).astype(F32)
    for x in range(4):
        for half in range(2):
            for ri in range(2):
                tile = sum_ref[ri, pl.ds(half * 8, 8), x] * keep
                slot = 2 * (x % 2) + ri
                turn_ref[slot, pl.ds(0, 64, stride=2), :] = tile[:, 0:8].reshape(64, LANES)
                turn_ref[slot, pl.ds(1, 64, stride=2), :] = tile[:, 8:16].reshape(64, LANES)
                block = turn_ref[slot].T
                for k in range(4):
                    out_ref[4 * k + x, pl.ds(ri * 64 + half, 32, stride=2), :] = block[k * 32 : k * 32 + 32]


def last_kernel(cells, cell_ref, gathered_ref, now_ref, old_ref, out_ref):
    def current(point):
        return gathered_ref[point : point + 1, :]

    out_ref[...] = next_vector(cell_ref, current, now_ref[...], old_ref[...], cells)


FIELD = (2, 16, 4, 16, LANES)
PIECES = (2, 16, 4, 16, WIDTH)
PARAMS = pltpu.CompilerParams(vmem_limit_bytes=24 * 2**20)


def local(
    orbitals,
    local_potential,
    projectors,
    strengths,
    material,
    proj_kind,
    point_cell,
    vector_now,
    vector_old,
):
    cells = vector_now.shape[0]
    shape = jax.ShapeDtypeStruct
    packed = pl.pallas_call(
        pack_kernel,
        out_shape=shape((GRID, PAYLOAD, LANES), F32),
        in_specs=[HBM] * 4,
        out_specs=VMEM,
        scratch_shapes=[
            pltpu.SMEM(proj_kind.shape, jnp.int32),
            pltpu.VMEM((16, LANES), F32),
            pltpu.SemaphoreType.DMA((2,)),
            pltpu.SemaphoreType.DMA((6 * LOCAL,)),
        ],
        compiler_params=PARAMS,
        name="pack",
    )(
        proj_kind,
        orbitals.reshape(2, LOCAL, 2, 64, LANES),
        projectors.reshape(2, 64, LANES),
        local_potential.reshape(16, LANES),
    )
    received = lax.all_to_all(packed, "grid", split_axis=0, concat_axis=0, tiled=True)
    other = lax.ppermute(received[:, 128:160], "grid", [(i, i ^ 1) for i in range(GRID)])
    field, pieces, diag = pl.pallas_call(
        unpack_kernel,
        out_shape=[shape(FIELD, F32), shape(PIECES, BF16), shape(FIELD[1:], F32)],
        in_specs=[VMEM],
        out_specs=[VMEM] * 3,
        scratch_shapes=[pltpu.VMEM((6, LANES, LANES), F32)],
        compiler_params=PARAMS,
        cost_estimate=pl.CostEstimate(flops=10**7, bytes_accessed=5 * 2**20, transcendentals=0),
        name="unpack",
    )(received)
    fields = [pltpu.VMEM(FIELD, F32)] * 2 + [pltpu.VMEM(PIECES, BF16)]
    working = [
        pltpu.VMEM((4, LANES, LANES), F32),
        pltpu.VMEM((16, 4, 16, WIDTH), F32),
        pltpu.VMEM((384, WIDTH), BF16),
    ]
    field, pieces, rows, columns, part = pl.pallas_call(
        first_kernel,
        out_shape=[
            shape(FIELD, F32),
            shape(PIECES, BF16),
            shape((16, 4, 16, 384), BF16),
            shape((256, 1024), BF16),
            shape((LANES, LANES), F32),
        ],
        in_specs=[SMEM] * 4 + [VMEM] * 6,
        out_specs=[VMEM] * 5,
        scratch_shapes=fields + [pltpu.VMEM(FIELD[1:], F32)] + working,
        compiler_params=PARAMS,
        name="first",
    )(proj_kind, point_cell, material, vector_now, strengths, received, other, field, pieces, diag)
    part = part.reshape(LANES, 1, LANES)
    part = lax.all_to_all(part, ("micro", "grid"), split_axis=0, concat_axis=0, tiled=True)
    macro = MACRO_ROWS * LANES
    now = jnp.pad(vector_now, (0, macro - cells)).reshape(MACRO_ROWS, LANES)
    old = jnp.pad(vector_old, (0, macro - cells)).reshape(MACRO_ROWS, LANES)
    out, following = pl.pallas_call(
        functools.partial(second_kernel, cells),
        out_shape=[shape((GRID, RETURN, LANES), F32), shape((MACRO_ROWS, LANES), F32)],
        in_specs=[SMEM] * 3 + [VMEM] * 9,
        out_specs=[VMEM] * 2,
        scratch_shapes=[pltpu.VMEM(FIELD, F32)] + fields + working,
        compiler_params=PARAMS,
        name="second",
    )(
        proj_kind, point_cell, material, strengths, part.reshape(LANES, LANES), now, old,
        field, pieces, diag, rows, columns,
    )
    out = lax.all_to_all(out, "grid", split_axis=0, concat_axis=0, tiled=True)
    part = jnp.sum(out[:, 128].reshape(LOCAL, 2, LANES), axis=1)
    part = lax.all_to_all(jnp.broadcast_to(part, (8, LOCAL, LANES)), "micro", split_axis=0, concat_axis=0, tiled=True)
    last = pl.pallas_call(
        functools.partial(last_kernel, cells),
        out_shape=shape((MACRO_ROWS, LANES), F32),
        in_specs=[SMEM] + [VMEM] * 3,
        out_specs=VMEM,
        compiler_params=PARAMS,
        name="last",
    )(point_cell, part.reshape(64, LANES), following, now)
    out = out[:, 0:128].reshape(LOCAL, 2, 2, 64, LANES).transpose(2, 0, 1, 3, 4)
    return out.reshape(orbitals.shape), last.reshape(macro)[:cells]


def solution(mesh):
    in_specs = (
        P(None, "micro", None, "grid", None),
        P("micro", "grid", None),
        P(None, None, "grid", None),
        P(),
        P(),
        P(),
        P(),
        P(),
        P(),
    )
    out_specs = (P(None, "micro", None, "grid", None), P())
    return jax.shard_map(local, mesh=mesh, in_specs=in_specs, out_specs=out_specs, check_vma=False)
```

```python
import functools

import jax
import jax.numpy as jnp
from jax import lax
from jax.experimental import pallas as pl
from jax.experimental.pallas import tpu as pltpu
from jax.sharding import PartitionSpec as P

ORB = 64
STEPS = 2
ORDER = 4
SPACING = 0.64
TIME_STEP = 0.05
COURANT = 0.9
COUPLING = 1.0

GRID = 16
LOCAL = 8
HALF = 32
CELLS = 4096
NPROJ = 32
LANES = 128
WIDTH = 2 * LANES
PAYLOAD = 162
RETURN = 130
MACRO_ROWS = 16
KINETIC = TIME_STEP / (2.0 * SPACING**2)
F32 = jnp.float32
BF16 = jnp.bfloat16
VMEM = pl.BlockSpec(memory_space=pltpu.VMEM)
SMEM = pl.BlockSpec(memory_space=pltpu.SMEM)
HBM = pl.BlockSpec(memory_space=pltpu.HBM)


def split(value):
    high = value.astype(BF16)
    low = (value - high.astype(F32)).astype(BF16)
    return high, low


def dot(a, b):
    return jnp.dot(a, b, preferred_element_type=F32)


def pack_kernel(kind_hbm, x_hbm, proj_hbm, pot_hbm, out_ref, kind_ref, sem):
    copies = []

    def start(source, target):
        copies.append(pltpu.make_async_copy(source, target, sem.at[len(copies)]))
        copies[-1].start()

    kind_copy = pltpu.make_async_copy(kind_hbm, kind_ref, sem.at[14])
    kind_copy.start()
    for ri in range(2):
        for part in range(2):
            points = pl.ds(part * 4, 4)
            start(x_hbm.at[ri, points], out_ref.at[points, :, pl.ds(ri * 32, 32)])
    for h in range(2):
        start(pot_hbm, out_ref.at[:, h, 80])
    kind_copy.wait()
    first = lax.axis_index("micro") * LOCAL
    for p in range(LOCAL):
        start(proj_hbm.at[kind_ref[first + p]], out_ref.at[p, :, pl.ds(64, 16)])
    for copy in copies:
        copy.wait()


def unpermute_kernel(recv_ref, out_hbm, sem):
    copies = []
    for ri in range(2):
        source = recv_ref.at[:, :, pl.ds(ri * 32, 32)]
        copies.append(pltpu.make_async_copy(source, out_hbm.at[ri], sem.at[ri]))
        copies[-1].start()
    for copy in copies:
        copy.wait()


def turned(block, turn_ref, slot):
    turn_ref[slot] = block.T
    even = turn_ref[slot, pl.ds(0, 64, stride=2), :].reshape(8, 8, LANES)
    odd = turn_ref[slot, pl.ds(1, 64, stride=2), :].reshape(8, 8, LANES)
    return jnp.concatenate([even, odd], axis=1)


def unpack_kernel(
    kind_ref, cell_ref, material_ref, vector_ref, strength_ref, recv_ref,
    u_ref, pieces_ref, diag_ref, small_ref, cells_ref, turn_ref,
):
    point = lax.axis_index("micro") * LOCAL + lax.axis_index("grid") // 2
    occupied = jnp.logical_or(lax.axis_index("grid") % 2 == 0, material_ref[point] == 1)
    small_ref[0:1, :] = jnp.full((1, LANES), vector_ref[cell_ref[point]], F32)
    small_ref[1:2, :] = jnp.full((1, LANES), jnp.where(occupied, 1.0, 0.0), F32)
    small_ref[2:8, :] = jnp.full((6, LANES), cell_ref[point].astype(F32), F32)
    small_ref[8:40, :] = jnp.broadcast_to(projector_weight(kind_ref[point], strength_ref), (NPROJ, LANES))
    for p in range(64):
        cells_ref[p : p + 1, :] = jnp.full((1, LANES), cell_ref[p], jnp.int32)
    for x in range(4):
        for half in range(2):
            y = pl.ds(half * 8, 8)
            for ri in range(2):
                block = []
                for k in range(4):
                    rows = pl.ds((4 * k + x) * PAYLOAD + ri * 64 + half, 32, stride=2)
                    block.append(recv_ref[rows, :])
                block = jnp.concatenate(block, axis=0)
                tile = turned(block, turn_ref, (2 * x + half) % 2 * 3 + ri)
                u_ref[ri, y, x] = tile
                high, low = split(tile)
                lanes = slice(ri * LANES, (ri + 1) * LANES)
                pieces_ref[0, y, x, :, lanes] = high
                pieces_ref[1, y, x, :, lanes] = low
            block = []
            for k in range(4):
                row = (4 * k + x) * PAYLOAD + 160 + half
                block.append(jnp.broadcast_to(recv_ref[row : row + 1, :], (32, LANES)))
            block = jnp.concatenate(block, axis=0)
            tile = turned(block, turn_ref, (2 * x + half) % 2 * 3 + 2)
            diag_ref[y, x] = TIME_STEP * (3.0 / SPACING**2 + tile)


def unpack_projectors(recv_ref, other_ref, beta_ref, rows_ref, columns_ref, turn_ref):
    for x in range(4):
        for half in range(2):
            y = pl.ds(half * 8, 8)
            block = []
            for k in range(4):
                block.append(recv_ref[pl.ds((4 * k + x) * PAYLOAD + 128 + half, 16, stride=2), :])
                block.append(other_ref[pl.ds((4 * k + x) * 32 + half, 16, stride=2), :])
            tile = turned(jnp.concatenate(block, axis=0), turn_ref, 2 * (x % 2) + half)
            beta_ref[y, x] = tile
            high, low = split(tile)
            rows_ref[y, x, :, 0:128] = high
            rows_ref[y, x, :, 128:256] = low
            rows_ref[y, x, :, 256:384] = high
    for b in range(8):
        block = beta_ref[2 * b : 2 * b + 2].reshape(LANES, LANES).T
        high, low = split(block)
        columns_ref[0:128, b * LANES : (b + 1) * LANES] = high
        columns_ref[128:256, b * LANES : (b + 1) * LANES] = low


def apply(scale, a, weight, u_ref, term_ref, out_ref, pieces_in, pieces_out, diag_ref, rows_ref, columns_ref, nonlocal_ref, coef_ref, current):
    diag_shift = TIME_STEP * 0.5 * a * a
    drift = a * (TIME_STEP / (2.0 * SPACING))
    group_of_lane = lax.broadcasted_iota(jnp.int32, (NPROJ, WIDTH), 1) % LANES // 32
    high = pieces_in[0].reshape(1024, WIDTH)
    low = pieces_in[1].reshape(1024, WIDTH)
    both = dot(columns_ref[...], high)
    coef = both[0:128] + both[128:256] + dot(columns_ref[0:128], low)
    mine = jnp.zeros((NPROJ, WIDTH), F32)
    for k in range(4):
        mine = mine + jnp.where(group_of_lane == k, coef[k * 32 : k * 32 + 32], 0.0)
    parts = []
    for ri in range(2):
        part = mine[:, ri * LANES : (ri + 1) * LANES]
        part = part + pltpu.roll(part, 64, 1)
        part = part + pltpu.roll(part, 32, 1)
        parts.append(part)
    mine = jnp.concatenate(parts, axis=1) * weight
    for k in range(4):
        high, low = split(jnp.where(group_of_lane == k, mine, 0.0))
        coef_ref[k * 32 : k * 32 + 32, :] = high
        coef_ref[128 + k * 32 : 128 + k * 32 + 32, :] = high
        coef_ref[256 + k * 32 : 256 + k * 32 + 32, :] = low

    def row(y, total):
        above = (y + 1) % 16
        below = (y + 15) % 16
        centre = [[term_ref[ri, y, x] for x in range(4)] for ri in range(2)]
        for x in range(4):
            diag = diag_ref[y, x] + diag_shift
            kinetic, gradient = [], []
            for ri in range(2):
                c = centre[ri][x]
                right = centre[ri][x + 1] if x < 3 else pltpu.roll(centre[ri][0], 96, 1)
                left = centre[ri][x - 1] if x > 0 else pltpu.roll(centre[ri][3], 32, 1)
                across = right + left + (term_ref[ri, above, x] + term_ref[ri, below, x])
                even, odd = c[0:8], c[8:16]
                before = pltpu.roll(odd, 1, 0)
                after = pltpu.roll(even, 7, 0)
                around = across + jnp.concatenate([odd + before, after + even], axis=0)
                gradient.append(jnp.concatenate([odd - before, after - even], axis=0))
                there = nonlocal_ref[y, x, :, ri * LANES : (ri + 1) * LANES]
                kinetic.append(diag * c - KINETIC * around + there)
            new = [
                u_ref[0, y, x] + scale * (kinetic[1] - drift * gradient[0]),
                u_ref[1, y, x] - scale * (kinetic[0] + drift * gradient[1]),
            ]
            for ri in range(2):
                out_ref[ri, y, x] = new[ri]
                if pieces_out is not None:
                    high, low = split(new[ri])
                    lanes = slice(ri * LANES, (ri + 1) * LANES)
                    pieces_out[0, y, x, :, lanes] = high
                    pieces_out[1, y, x, :, lanes] = low
            if current:
                real, imag = new
                real_even, real_odd = real[0:8], real[8:16]
                imag_even, imag_odd = imag[0:8], imag[8:16]
                flow = real_even * imag_odd - imag_even * real_odd
                flow = flow + (real_odd * pltpu.roll(imag_even, 7, 0) - imag_odd * pltpu.roll(real_even, 7, 0))
                square = real * real + imag * imag
                total = total + (flow * (1.0 / SPACING) + a * (square[0:8] + square[8:16]))
        return total

    for chunk in range(4):
        ys = pl.ds(4 * chunk, 4)
        nonlocal_ref[ys] = dot(rows_ref[ys].reshape(256, 384), coef_ref[...]).reshape(4, 4, 16, WIDTH)
    total = jnp.zeros((8, LANES), F32)
    for y in range(16):
        total = row(y, total)
    if current:
        total = jnp.sum(jnp.sum(total, axis=0, keepdims=True), axis=1, keepdims=True)
        return total * (2.0 / (ORB * CELLS))


def propagate(a, weight, u_ref, out_ref, pieces_first, term_refs, pieces_ref, *others):
    one, two = term_refs
    apply(1.0 / 4, a, weight, u_ref, u_ref, one, pieces_first, pieces_ref, *others, False)
    apply(1.0 / 3, a, weight, u_ref, one, two, pieces_ref, pieces_ref, *others, False)
    apply(1.0 / 2, a, weight, u_ref, two, one, pieces_ref, pieces_ref, *others, False)
    return apply(1.0, a, weight, u_ref, one, out_ref, pieces_ref, None, *others, True)


def projector_weight(kind, strength_ref):
    row = jnp.where(kind == 0, strength_ref[0:1, :], strength_ref[1:2, :])
    across = lax.broadcasted_iota(jnp.int32, (NPROJ, NPROJ), 1)
    down = lax.broadcasted_iota(jnp.int32, (NPROJ, NPROJ), 0)
    down = (down + lax.axis_index("grid") % 2 * (NPROJ // 2)) % NPROJ
    return TIME_STEP * jnp.sum(jnp.where(across == down, row, 0.0), axis=1, keepdims=True)


def doubled(weight):
    return jnp.concatenate([weight, weight], axis=1)


def first_kernel(
    small_ref, recv_ref, other_ref, u_ref, pieces_in, diag_ref,
    out_ref, rows_ref, columns_ref, part_ref,
    one_ref, two_ref, pieces_ref, beta_ref, turn_ref, nonlocal_ref, coef_ref,
):
    unpack_projectors(recv_ref, other_ref, beta_ref, rows_ref, columns_ref, turn_ref)
    a = small_ref[0:1, :]
    weight = doubled(small_ref[8:40, :])
    others = (diag_ref, rows_ref, columns_ref, nonlocal_ref, coef_ref)
    part = propagate(a, weight, u_ref, out_ref, pieces_in, (one_ref, two_ref), pieces_ref, *others)
    part_ref[...] = jnp.broadcast_to(part * small_ref[1:2, :], (LANES, LANES))


def macro_index():
    down = lax.broadcasted_iota(jnp.int32, (MACRO_ROWS, LANES), 0)
    return down * LANES + lax.broadcasted_iota(jnp.int32, (MACRO_ROWS, LANES), 1)


def next_vector(cells_ref, current, present, previous, cells):
    index = macro_index()
    deposit = jnp.zeros((MACRO_ROWS, LANES), F32)
    for point in range(64):
        deposit = deposit + jnp.where(index == cells_ref[point : point + 1, :], current(point), 0.0)
    lane = lax.broadcasted_iota(jnp.int32, (MACRO_ROWS, LANES), 1)
    zero_row = jnp.zeros((1, LANES), F32)
    back = pltpu.roll(present, 1, 1)
    back = jnp.where(lane == 0, jnp.concatenate([zero_row, back[:-1]], axis=0), back)
    forth = pltpu.roll(present, LANES - 1, 1)
    forth = jnp.where(lane == LANES - 1, jnp.concatenate([forth[1:], zero_row], axis=0), forth)
    curvature = forth + back - 2.0 * present
    following = 2.0 * present - previous + COURANT**2 * curvature - COUPLING * deposit
    return jnp.where(index < cells, following, 0.0)


def second_kernel(
    cells,
    small_ref, cells_ref, gathered_ref, now_ref, old_ref, u_ref, diag_ref, rows_ref, columns_ref,
    out_ref, vector_ref,
    sum_ref, one_ref, two_ref, pieces_ref, turn_ref, nonlocal_ref, coef_ref,
):
    def current(point):
        return gathered_ref[2 * point : 2 * point + 1, :] + gathered_ref[2 * point + 1 : 2 * point + 2, :]

    for ri in range(2):
        for y in range(16):
            high, low = split(u_ref[ri, y])
            pieces_ref[0, y, :, :, ri * LANES : (ri + 1) * LANES] = high
            pieces_ref[1, y, :, :, ri * LANES : (ri + 1) * LANES] = low
    following = next_vector(cells_ref, current, now_ref[...], old_ref[...], cells)
    vector_ref[...] = following
    mine = jnp.where(macro_index().astype(F32) == small_ref[2:3, :], following, 0.0)
    a = jnp.sum(jnp.sum(mine, axis=0, keepdims=True), axis=1, keepdims=True)
    weight = doubled(small_ref[8:40, :])
    others = (diag_ref, rows_ref, columns_ref, nonlocal_ref, coef_ref)
    part = propagate(a, weight, u_ref, sum_ref, pieces_ref, (one_ref, two_ref), pieces_ref, *others)
    keep = small_ref[1:2, :]
    for g in range(GRID):
        out_ref[g * RETURN + 128 : (g + 1) * RETURN, :] = jnp.broadcast_to(part * keep, (2, LANES))
    for x in range(4):
        for half in range(2):
            for ri in range(2):
                tile = sum_ref[ri, pl.ds(half * 8, 8), x] * keep
                slot = 2 * (x % 2) + ri
                turn_ref[slot, pl.ds(0, 64, stride=2), :] = tile[:, 0:8].reshape(64, LANES)
                turn_ref[slot, pl.ds(1, 64, stride=2), :] = tile[:, 8:16].reshape(64, LANES)
                block = turn_ref[slot].T
                for k in range(4):
                    rows = pl.ds((4 * k + x) * RETURN + ri * 64 + half, 32, stride=2)
                    out_ref[rows, :] = block[k * 32 : k * 32 + 32]


def last_kernel(cells, cells_ref, gathered_ref, now_ref, old_ref, out_ref):
    def current(point):
        return gathered_ref[point : point + 1, :]

    out_ref[...] = next_vector(cells_ref, current, now_ref[...], old_ref[...], cells)


FIELD = (2, 16, 4, 16, LANES)
PIECES = (2, 16, 4, 16, WIDTH)
PARAMS = pltpu.CompilerParams(vmem_limit_bytes=24 * 2**20)


def local(
    orbitals,
    local_potential,
    projectors,
    strengths,
    material,
    proj_kind,
    point_cell,
    vector_now,
    vector_old,
):
    cells = vector_now.shape[0]
    shape = jax.ShapeDtypeStruct

    def in_hbm(array, *dims):
        return pltpu.with_memory_space_constraint(array.reshape(dims), pltpu.HBM)

    packed = pl.pallas_call(
        pack_kernel,
        out_shape=shape((LOCAL, 2, PAYLOAD // 2, 2, LANES), F32),
        in_specs=[HBM] * 4,
        out_specs=VMEM,
        scratch_shapes=[pltpu.SMEM(proj_kind.shape, jnp.int32), pltpu.SemaphoreType.DMA((15,))],
        compiler_params=PARAMS,
        name="pack",
    )(
        in_hbm(proj_kind, 64),
        in_hbm(orbitals, 2, LOCAL, 2, 32, 2, LANES),
        in_hbm(projectors, 2, 2, 16, 2, LANES),
        in_hbm(local_potential, LOCAL, 2, LANES),
    )
    packed = packed.reshape(GRID, PAYLOAD // 2, 2, LANES)
    received = lax.all_to_all(packed, "grid", split_axis=0, concat_axis=0, tiled=True)
    other = lax.ppermute(received[:, 64:80], "grid", [(i, i ^ 1) for i in range(GRID)])
    other = other.reshape(GRID * 32, LANES)
    received = received.reshape(GRID * PAYLOAD, LANES)
    field, pieces, diag, small, cell_rows = pl.pallas_call(
        unpack_kernel,
        out_shape=[
            shape(FIELD, F32),
            shape(PIECES, BF16),
            shape(FIELD[1:], F32),
            shape((40, LANES), F32),
            shape((64, LANES), jnp.int32),
        ],
        in_specs=[SMEM] * 4 + [VMEM] * 2,
        out_specs=[VMEM] * 5,
        scratch_shapes=[pltpu.VMEM((6, LANES, LANES), F32)],
        compiler_params=PARAMS,
        cost_estimate=pl.CostEstimate(flops=10**7, bytes_accessed=5 * 2**20, transcendentals=0),
        name="unpack",
    )(proj_kind, point_cell, material, vector_now, strengths, received)
    fields = [pltpu.VMEM(FIELD, F32)] * 2 + [pltpu.VMEM(PIECES, BF16)]
    working = [
        pltpu.VMEM((4, LANES, LANES), F32),
        pltpu.VMEM((16, 4, 16, WIDTH), F32),
        pltpu.VMEM((384, WIDTH), BF16),
    ]
    field, rows, columns, part = pl.pallas_call(
        first_kernel,
        out_shape=[
            shape(FIELD, F32),
            shape((16, 4, 16, 384), BF16),
            shape((256, 1024), BF16),
            shape((LANES, LANES), F32),
        ],
        in_specs=[VMEM] * 6,
        out_specs=[VMEM] * 4,
        scratch_shapes=fields + [pltpu.VMEM(FIELD[1:], F32)] + working,
        compiler_params=PARAMS,
        name="first",
    )(small, received, other, field, pieces, diag)
    part = part.reshape(LANES, 1, LANES)
    part = lax.all_to_all(part, ("micro", "grid"), split_axis=0, concat_axis=0, tiled=True)
    macro = MACRO_ROWS * LANES
    now = jnp.pad(vector_now, (0, macro - cells)).reshape(MACRO_ROWS, LANES)
    old = jnp.pad(vector_old, (0, macro - cells)).reshape(MACRO_ROWS, LANES)
    out, following = pl.pallas_call(
        functools.partial(second_kernel, cells),
        out_shape=[shape((GRID * RETURN, LANES), F32), shape((MACRO_ROWS, LANES), F32)],
        in_specs=[VMEM] * 9,
        out_specs=[VMEM] * 2,
        scratch_shapes=[pltpu.VMEM(FIELD, F32)] + fields + working,
        compiler_params=PARAMS,
        name="second",
    )(small, cell_rows, part.reshape(LANES, LANES), now, old, field, diag, rows, columns)
    out = out.reshape(GRID, RETURN // 2, 2, LANES)
    out = lax.all_to_all(out, "grid", split_axis=0, concat_axis=0, tiled=True)
    part = jnp.sum(out[:, 64, 0].reshape(LOCAL, 2, LANES), axis=1)
    part = lax.all_to_all(jnp.broadcast_to(part, (8, LOCAL, LANES)), "micro", split_axis=0, concat_axis=0, tiled=True)
    out = pl.pallas_call(
        unpermute_kernel,
        out_shape=pltpu.HBM((2, LOCAL, 2, 32, 2, LANES), F32),
        in_specs=[VMEM],
        out_specs=HBM,
        scratch_shapes=[pltpu.SemaphoreType.DMA((2,))],
        compiler_params=PARAMS,
        cost_estimate=pl.CostEstimate(flops=10**6, bytes_accessed=2 * 2**20, transcendentals=0),
        name="unpermute",
    )(out.reshape(LOCAL, 2, RETURN // 2, 2, LANES))
    last = pl.pallas_call(
        functools.partial(last_kernel, cells),
        out_shape=shape((MACRO_ROWS, LANES), F32),
        in_specs=[VMEM] * 4,
        out_specs=VMEM,
        compiler_params=PARAMS,
        name="last",
    )(cell_rows, part.reshape(64, LANES), following, now)
    return out.reshape(orbitals.shape), last.reshape(macro)[:cells]


def solution(mesh):
    in_specs = (
        P(None, "micro", None, "grid", None),
        P("micro", "grid", None),
        P(None, None, "grid", None),
        P(),
        P(),
        P(),
        P(),
        P(),
        P(),
    )
    out_specs = (P(None, "micro", None, "grid", None), P())
    return jax.shard_map(local, mesh=mesh, in_specs=in_specs, out_specs=out_specs, check_vma=False)
```

```python
import functools

import jax
import jax.numpy as jnp
from jax import lax
from jax.experimental import pallas as pl
from jax.experimental.pallas import tpu as pltpu
from jax.sharding import PartitionSpec as P

ORB = 64
STEPS = 2
ORDER = 4
SPACING = 0.64
TIME_STEP = 0.05
COURANT = 0.9
COUPLING = 1.0

GRID = 16
LOCAL = 8
HALF = 32
CELLS = 4096
NPROJ = 32
LANES = 128
WIDTH = 2 * LANES
PAYLOAD = 162
RETURN = 130
MACRO_ROWS = 16
KINETIC = TIME_STEP / (2.0 * SPACING**2)
F32 = jnp.float32
BF16 = jnp.bfloat16
VMEM = pl.BlockSpec(memory_space=pltpu.VMEM)
SMEM = pl.BlockSpec(memory_space=pltpu.SMEM)
HBM = pl.BlockSpec(memory_space=pltpu.HBM)


def split(value):
    high = value.astype(BF16)
    low = (value - high.astype(F32)).astype(BF16)
    return high, low


def dot(a, b):
    return jnp.dot(a, b, preferred_element_type=F32)


def pack_kernel(kind_hbm, x_hbm, proj_hbm, pot_hbm, out_ref, kind_ref, proj_ref, sem):
    copies = []

    def start(source, target):
        copies.append(pltpu.make_async_copy(source, target, sem.at[len(copies)]))
        copies[-1].start()

    kind_copy = pltpu.make_async_copy(kind_hbm, kind_ref, sem.at[6])
    kind_copy.start()
    proj_copy = pltpu.make_async_copy(proj_hbm, proj_ref, sem.at[7])
    proj_copy.start()
    for ri in range(2):
        for part in range(2):
            points = pl.ds(part * 4, 4)
            start(x_hbm.at[ri, points], out_ref.at[points, :, pl.ds(ri * 32, 32)])
    for h in range(2):
        start(pot_hbm, out_ref.at[:, h, 80])
    kind_copy.wait()
    proj_copy.wait()
    first = lax.axis_index("micro") * LOCAL
    for p in range(LOCAL):
        out_ref[p, :, 64:80] = proj_ref[kind_ref[first + p]]
    for copy in copies:
        copy.wait()


def unpermute_kernel(recv_ref, out_hbm, sem):
    copies = []
    for ri in range(2):
        source = recv_ref.at[:, :, pl.ds(ri * 32, 32)]
        copies.append(pltpu.make_async_copy(source, out_hbm.at[ri], sem.at[ri]))
        copies[-1].start()
    for copy in copies:
        copy.wait()


def turned(block, turn_ref, slot):
    turn_ref[slot] = block.T
    even = turn_ref[slot, pl.ds(0, 64, stride=2), :].reshape(8, 8, LANES)
    odd = turn_ref[slot, pl.ds(1, 64, stride=2), :].reshape(8, 8, LANES)
    return jnp.concatenate([even, odd], axis=1)


def unpack_kernel(
    kind_ref, cell_ref, material_ref, now_ref, old_ref, cell_row_ref, strength_ref, recv_ref,
    u_ref, pieces_ref, diag_ref, small_ref, cells_ref, same_ref, equal_ref, turn_ref,
):
    point = lax.axis_index("micro") * LOCAL + lax.axis_index("grid") // 2
    occupied = jnp.logical_or(lax.axis_index("grid") % 2 == 0, material_ref[point] == 1)
    cell = cell_ref[point]
    cells = now_ref.shape[0]

    def row(scalar):
        return jnp.full((1, LANES), scalar)

    here = row(now_ref[cell])
    back = row(jnp.where(cell == 0, 0.0, now_ref[jnp.maximum(cell - 1, 0)]))
    forth = row(jnp.where(cell == cells - 1, 0.0, now_ref[jnp.minimum(cell + 1, cells - 1)]))
    small_ref[0:1, :] = here
    small_ref[1:2, :] = row(jnp.where(occupied, 1.0, 0.0))
    small_ref[2:3, :] = 2.0 * here - row(old_ref[cell]) + COURANT**2 * (forth + back - 2.0 * here)
    small_ref[8:40, :] = jnp.broadcast_to(projector_weight(kind_ref[point], strength_ref), (NPROJ, LANES))
    for p in range(64):
        cells_ref[p : p + 1, :] = row(cell_ref[p])
        same_ref[p : p + 1, :] = row(jnp.where(cell_ref[p] == cell, 1.0, 0.0))
    equal = jnp.where(cells_ref[:, 0:64] == cell_row_ref[...], 1.0, 0.0)
    equal_ref[0] = jnp.sum(equal).astype(jnp.int32)
    small_ref[3:8, :] = jnp.zeros((5, LANES), F32)
    for x in range(4):
        for half in range(2):
            y = pl.ds(half * 8, 8)
            for ri in range(2):
                block = []
                for k in range(4):
                    rows = pl.ds((4 * k + x) * PAYLOAD + ri * 64 + half, 32, stride=2)
                    block.append(recv_ref[rows, :])
                block = jnp.concatenate(block, axis=0)
                tile = turned(block, turn_ref, (2 * x + half) % 2 * 3 + ri)
                u_ref[ri, y, x] = tile
                high, low = split(tile)
                lanes = slice(ri * LANES, (ri + 1) * LANES)
                pieces_ref[0, y, x, :, lanes] = high
                pieces_ref[1, y, x, :, lanes] = low
            block = []
            for k in range(4):
                row = (4 * k + x) * PAYLOAD + 160 + half
                block.append(jnp.broadcast_to(recv_ref[row : row + 1, :], (32, LANES)))
            block = jnp.concatenate(block, axis=0)
            tile = turned(block, turn_ref, (2 * x + half) % 2 * 3 + 2)
            diag_ref[y, x] = TIME_STEP * (3.0 / SPACING**2 + tile)


def unpack_projectors(recv_ref, other_ref, beta_ref, rows_ref, columns_ref, turn_ref):
    for x in range(4):
        for half in range(2):
            y = pl.ds(half * 8, 8)
            block = []
            for k in range(4):
                block.append(recv_ref[pl.ds((4 * k + x) * PAYLOAD + 128 + half, 16, stride=2), :])
                block.append(other_ref[pl.ds((4 * k + x) * 32 + half, 16, stride=2), :])
            tile = turned(jnp.concatenate(block, axis=0), turn_ref, 2 * (x % 2) + half)
            beta_ref[y, x] = tile
            high, low = split(tile)
            rows_ref[y, x, :, 0:128] = high
            rows_ref[y, x, :, 128:256] = low
            rows_ref[y, x, :, 256:384] = high
    for b in range(8):
        block = beta_ref[2 * b : 2 * b + 2].reshape(LANES, LANES).T
        high, low = split(block)
        columns_ref[0:128, b * LANES : (b + 1) * LANES] = high
        columns_ref[128:256, b * LANES : (b + 1) * LANES] = low


def apply(scale, a, weight, u_ref, term_ref, out_ref, pieces_in, pieces_out, diag_ref, rows_ref, columns_ref, nonlocal_ref, coef_ref, current):
    diag_shift = TIME_STEP * 0.5 * a * a
    drift = a * (TIME_STEP / (2.0 * SPACING))
    group_of_lane = lax.broadcasted_iota(jnp.int32, (NPROJ, WIDTH), 1) % LANES // 32
    high = pieces_in[0].reshape(1024, WIDTH)
    low = pieces_in[1].reshape(1024, WIDTH)
    both = dot(columns_ref[...], high)
    coef = both[0:128] + both[128:256] + dot(columns_ref[0:128], low)
    def stencil(y, x, centre):
        diag = scale * diag_ref[y, x] + scale * diag_shift
        above = (y + 1) % 16
        below = (y + 15) % 16
        kinetic, gradient = [], []
        for ri in range(2):
            c = centre[ri][x]
            right = centre[ri][x + 1] if x < 3 else pltpu.roll(centre[ri][0], 96, 1)
            left = centre[ri][x - 1] if x > 0 else pltpu.roll(centre[ri][3], 32, 1)
            across = right + left + (term_ref[ri, above, x] + term_ref[ri, below, x])
            even, odd = c[0:8], c[8:16]
            before = pltpu.roll(odd, 1, 0)
            after = pltpu.roll(even, 7, 0)
            around = across + jnp.concatenate([odd + before, after + even], axis=0)
            gradient.append(jnp.concatenate([odd - before, after - even], axis=0))
            kinetic.append(diag * c - (scale * KINETIC) * around)
        real = u_ref[0, y, x] + (kinetic[1] - scale * drift * gradient[0])
        imag = u_ref[1, y, x] - (kinetic[0] + scale * drift * gradient[1])
        return real, imag

    def finish(y, x, real, imag, total):
        new = [real + nonlocal_ref[y, x, :, LANES:WIDTH], imag - nonlocal_ref[y, x, :, 0:LANES]]
        for ri in range(2):
            out_ref[ri, y, x] = new[ri]
            if pieces_out is not None:
                high, low = split(new[ri])
                lanes = slice(ri * LANES, (ri + 1) * LANES)
                pieces_out[0, y, x, :, lanes] = high
                pieces_out[1, y, x, :, lanes] = low
        if current:
            real, imag = new
            real_even, real_odd = real[0:8], real[8:16]
            imag_even, imag_odd = imag[0:8], imag[8:16]
            flow = real_even * imag_odd - imag_even * real_odd
            flow = flow + (real_odd * pltpu.roll(imag_even, 7, 0) - imag_odd * pltpu.roll(real_even, 7, 0))
            square = real * real + imag * imag
            total = total + (flow * (1.0 / SPACING) + a * (square[0:8] + square[8:16]))
        return total

    mine = jnp.zeros((NPROJ, WIDTH), F32)
    for k in range(4):
        mine = mine + jnp.where(group_of_lane == k, coef[k * 32 : k * 32 + 32], 0.0)
    parts = []
    for ri in range(2):
        part = mine[:, ri * LANES : (ri + 1) * LANES]
        part = part + pltpu.roll(part, 64, 1)
        part = part + pltpu.roll(part, 32, 1)
        parts.append(part)
    mine = jnp.concatenate(parts, axis=1) * (scale * weight)
    for k in range(4):
        high, low = split(jnp.where(group_of_lane == k, mine, 0.0))
        coef_ref[k * 32 : k * 32 + 32, :] = high
        coef_ref[128 + k * 32 : 128 + k * 32 + 32, :] = high
        coef_ref[256 + k * 32 : 256 + k * 32 + 32, :] = low

    for chunk in range(4):
        ys = pl.ds(4 * chunk, 4)
        nonlocal_ref[ys] = dot(rows_ref[ys].reshape(256, 384), coef_ref[...]).reshape(4, 4, 16, WIDTH)
    total = jnp.zeros((8, LANES), F32)
    for y in range(16):
        centre = [[term_ref[ri, y, x] for x in range(4)] for ri in range(2)]
        for x in range(4):
            real, imag = stencil(y, x, centre)
            total = finish(y, x, real, imag, total)
    if current:
        total = jnp.sum(jnp.sum(total, axis=0, keepdims=True), axis=1, keepdims=True)
        return total * (2.0 / (ORB * CELLS))


def propagate(a, weight, u_ref, out_ref, pieces_first, term_refs, pieces_ref, *others):
    one, two = term_refs
    apply(1.0 / 4, a, weight, u_ref, u_ref, one, pieces_first, pieces_ref, *others, False)
    apply(1.0 / 3, a, weight, u_ref, one, two, pieces_ref, pieces_ref, *others, False)
    apply(1.0 / 2, a, weight, u_ref, two, one, pieces_ref, pieces_ref, *others, False)
    return apply(1.0, a, weight, u_ref, one, out_ref, pieces_ref, None, *others, True)


def projector_weight(kind, strength_ref):
    row = jnp.where(kind == 0, strength_ref[0:1, :], strength_ref[1:2, :])
    across = lax.broadcasted_iota(jnp.int32, (NPROJ, NPROJ), 1)
    down = lax.broadcasted_iota(jnp.int32, (NPROJ, NPROJ), 0)
    down = (down + lax.axis_index("grid") % 2 * (NPROJ // 2)) % NPROJ
    return TIME_STEP * jnp.sum(jnp.where(across == down, row, 0.0), axis=1, keepdims=True)


def doubled(weight):
    return jnp.concatenate([weight, weight], axis=1)


def first_kernel(
    small_ref, recv_ref, other_ref, u_ref, pieces_in, diag_ref,
    out_ref, rows_ref, columns_ref, part_ref,
    one_ref, two_ref, pieces_ref, beta_ref, turn_ref, nonlocal_ref, coef_ref,
):
    unpack_projectors(recv_ref, other_ref, beta_ref, rows_ref, columns_ref, turn_ref)
    a = small_ref[0:1, :]
    weight = doubled(small_ref[8:40, :])
    others = (diag_ref, rows_ref, columns_ref, nonlocal_ref, coef_ref)
    part = propagate(a, weight, u_ref, out_ref, pieces_in, (one_ref, two_ref), pieces_ref, *others)
    part_ref[...] = jnp.broadcast_to(part * small_ref[1:2, :], (LANES, LANES))


def macro_index():
    down = lax.broadcasted_iota(jnp.int32, (MACRO_ROWS, LANES), 0)
    return down * LANES + lax.broadcasted_iota(jnp.int32, (MACRO_ROWS, LANES), 1)


def next_vector(cells_ref, current, present, previous, cells):
    index = macro_index()
    deposit = jnp.zeros((MACRO_ROWS, LANES), F32)
    for point in range(64):
        deposit = deposit + jnp.where(index == cells_ref[point : point + 1, :], current(point), 0.0)
    lane = lax.broadcasted_iota(jnp.int32, (MACRO_ROWS, LANES), 1)
    zero_row = jnp.zeros((1, LANES), F32)
    back = pltpu.roll(present, 1, 1)
    back = jnp.where(lane == 0, jnp.concatenate([zero_row, back[:-1]], axis=0), back)
    forth = pltpu.roll(present, LANES - 1, 1)
    forth = jnp.where(lane == LANES - 1, jnp.concatenate([forth[1:], zero_row], axis=0), forth)
    curvature = forth + back - 2.0 * present
    following = 2.0 * present - previous + COURANT**2 * curvature - COUPLING * deposit
    return jnp.where(index < cells, following, 0.0)


def second_kernel(
    small_ref, deposit_ref, part_ref, u_ref, diag_ref, rows_ref, columns_ref,
    out_ref,
    sum_ref, one_ref, two_ref, pieces_ref, turn_ref, nonlocal_ref, coef_ref,
):
    for ri in range(2):
        for y in range(16):
            high, low = split(u_ref[ri, y])
            pieces_ref[0, y, :, :, ri * LANES : (ri + 1) * LANES] = high
            pieces_ref[1, y, :, :, ri * LANES : (ri + 1) * LANES] = low
    a = small_ref[2:3, :] - COUPLING * deposit_ref[0:1, :]
    weight = doubled(small_ref[8:40, :])
    others = (diag_ref, rows_ref, columns_ref, nonlocal_ref, coef_ref)
    part = propagate(a, weight, u_ref, sum_ref, pieces_ref, (one_ref, two_ref), pieces_ref, *others)
    keep = small_ref[1:2, :]
    for g in range(GRID):
        out_ref[g * RETURN + 128 : g * RETURN + 129, :] = part * keep
        out_ref[g * RETURN + 129 : g * RETURN + 130, :] = part_ref[0:1, :]
    for x in range(4):
        for half in range(2):
            for ri in range(2):
                tile = sum_ref[ri, pl.ds(half * 8, 8), x] * keep
                slot = 2 * (x % 2) + ri
                turn_ref[slot, pl.ds(0, 64, stride=2), :] = tile[:, 0:8].reshape(64, LANES)
                turn_ref[slot, pl.ds(1, 64, stride=2), :] = tile[:, 8:16].reshape(64, LANES)
                block = turn_ref[slot].T
                for k in range(4):
                    rows = pl.ds((4 * k + x) * RETURN + ri * 64 + half, 32, stride=2)
                    out_ref[rows, :] = block[k * 32 : k * 32 + 32]


def spread_kernel(recv_ref, out_ref):
    part = recv_ref[:, 0, 64] + recv_ref[:, 1, 64]
    for m in range(8):
        out_ref[m] = part


def last_kernel(cells, cells_ref, gathered_ref, now_ref, old_ref, out_ref):
    previous, present = old_ref[...], now_ref[...]
    for second in range(2):

        def current(point):
            row = 2 * point + 1 - second
            return gathered_ref[row : row + 1, :]

        previous, present = present, next_vector(cells_ref, current, present, previous, cells)
    out_ref[...] = present


FIELD = (2, 16, 4, 16, LANES)
PIECES = (2, 16, 4, 16, WIDTH)
PARAMS = pltpu.CompilerParams(vmem_limit_bytes=24 * 2**20)


def local(
    orbitals,
    local_potential,
    projectors,
    strengths,
    material,
    proj_kind,
    point_cell,
    vector_now,
    vector_old,
):
    cells = vector_now.shape[0]
    shape = jax.ShapeDtypeStruct

    def in_hbm(array, *dims):
        return pltpu.with_memory_space_constraint(array.reshape(dims), pltpu.HBM)

    packed = pl.pallas_call(
        pack_kernel,
        out_shape=shape((LOCAL, 2, PAYLOAD // 2, 2, LANES), F32),
        in_specs=[HBM] * 4,
        out_specs=VMEM,
        scratch_shapes=[
            pltpu.SMEM(proj_kind.shape, jnp.int32),
            pltpu.VMEM((2, 2, 16, 2, LANES), F32),
            pltpu.SemaphoreType.DMA((8,)),
        ],
        compiler_params=PARAMS,
        name="pack",
    )(
        in_hbm(proj_kind, 64),
        in_hbm(orbitals, 2, LOCAL, 2, 32, 2, LANES),
        in_hbm(projectors, 2, 2, 16, 2, LANES),
        in_hbm(local_potential, LOCAL, 2, LANES),
    )
    packed = packed.reshape(GRID, PAYLOAD // 2, 2, LANES)
    received = lax.all_to_all(packed, "grid", split_axis=0, concat_axis=0, tiled=True)
    other = lax.ppermute(received[:, 64:80], "grid", [(i, i ^ 1) for i in range(GRID)])
    other = other.reshape(GRID * 32, LANES)
    received = received.reshape(GRID * PAYLOAD, LANES)
    field, pieces, diag, small, cell_rows, same, equal = pl.pallas_call(
        unpack_kernel,
        out_shape=[
            shape(FIELD, F32),
            shape(PIECES, BF16),
            shape(FIELD[1:], F32),
            shape((40, LANES), F32),
            shape((64, LANES), jnp.int32),
            shape((64, LANES), F32),
            shape((1,), jnp.int32),
        ],
        in_specs=[SMEM] * 5 + [VMEM] * 3,
        out_specs=[VMEM] * 6 + [SMEM],
        scratch_shapes=[pltpu.VMEM((6, LANES, LANES), F32)],
        compiler_params=PARAMS,
        cost_estimate=pl.CostEstimate(flops=10**7, bytes_accessed=5 * 2**20, transcendentals=0),
        name="unpack",
    )(proj_kind, point_cell, material, vector_now, vector_old, point_cell.reshape(1, 64), strengths, received)
    fields = [pltpu.VMEM(FIELD, F32)] * 2 + [pltpu.VMEM(PIECES, BF16)]
    working = [
        pltpu.VMEM((4, LANES, LANES), F32),
        pltpu.VMEM((16, 4, 16, WIDTH), F32),
        pltpu.VMEM((384, WIDTH), BF16),
    ]
    field, rows, columns, part = pl.pallas_call(
        first_kernel,
        out_shape=[
            shape(FIELD, F32),
            shape((16, 4, 16, 384), BF16),
            shape((256, 1024), BF16),
            shape((LANES, LANES), F32),
        ],
        in_specs=[VMEM] * 6,
        out_specs=[VMEM] * 4,
        scratch_shapes=fields + [pltpu.VMEM(FIELD[1:], F32)] + working,
        compiler_params=PARAMS,
        name="first",
    )(small, received, other, field, pieces, diag)

    def own(part):
        part = part[0:8]
        return part + lax.ppermute(part, "grid", [(i, i ^ 1) for i in range(GRID)])

    def shared(part):
        part = part.reshape(LANES, 1, LANES)
        part = lax.all_to_all(part, ("micro", "grid"), split_axis=0, concat_axis=0, tiled=True)
        part = part.reshape(64, 2, LANES) * same[:, None, :]
        return jnp.broadcast_to(jnp.sum(part, axis=(0, 1)), (8, LANES))

    deposit = lax.cond(equal[0] == 64, own, shared, part)
    macro = MACRO_ROWS * LANES
    now = jnp.pad(vector_now, (0, macro - cells)).reshape(MACRO_ROWS, LANES)
    old = jnp.pad(vector_old, (0, macro - cells)).reshape(MACRO_ROWS, LANES)
    out = pl.pallas_call(
        second_kernel,
        out_shape=shape((GRID * RETURN, LANES), F32),
        in_specs=[VMEM] * 7,
        out_specs=VMEM,
        scratch_shapes=[pltpu.VMEM(FIELD, F32)] + fields + working,
        compiler_params=PARAMS,
        name="second",
    )(small, deposit, part, field, diag, rows, columns)
    out = out.reshape(GRID, RETURN // 2, 2, LANES)
    out = lax.all_to_all(out, "grid", split_axis=0, concat_axis=0, tiled=True)
    part = pl.pallas_call(
        spread_kernel,
        out_shape=shape((8, LOCAL, 2, LANES), F32),
        in_specs=[VMEM],
        out_specs=VMEM,
        compiler_params=PARAMS,
        name="spread",
    )(out.reshape(LOCAL, 2, RETURN // 2, 2, LANES))
    part = lax.all_to_all(part, "micro", split_axis=0, concat_axis=0, tiled=True)
    out = pl.pallas_call(
        unpermute_kernel,
        out_shape=pltpu.HBM((2, LOCAL, 2, 32, 2, LANES), F32),
        in_specs=[VMEM],
        out_specs=HBM,
        scratch_shapes=[pltpu.SemaphoreType.DMA((2,))],
        compiler_params=PARAMS,
        cost_estimate=pl.CostEstimate(flops=10**6, bytes_accessed=2 * 2**20, transcendentals=0),
        name="unpermute",
    )(out.reshape(LOCAL, 2, RETURN // 2, 2, LANES))
    last = pl.pallas_call(
        functools.partial(last_kernel, cells),
        out_shape=shape((MACRO_ROWS, LANES), F32),
        in_specs=[VMEM] * 4,
        out_specs=VMEM,
        compiler_params=PARAMS,
        name="last",
    )(cell_rows, part.reshape(LANES, LANES), now, old)
    return out.reshape(orbitals.shape), last.reshape(macro)[:cells]


def solution(mesh):
    in_specs = (
        P(None, "micro", None, "grid", None),
        P("micro", "grid", None),
        P(None, None, "grid", None),
        P(),
        P(),
        P(),
        P(),
        P(),
        P(),
    )
    out_specs = (P(None, "micro", None, "grid", None), P())
    return jax.shard_map(local, mesh=mesh, in_specs=in_specs, out_specs=out_specs, check_vma=False)
```
